32 devices in a mesh: groups: 2 (over y), weight: 4 (over x, core), dp: 4 (over z).
Axes of the slice: x: 2, y: 2, z: 4, core: 2. Of those that a mesh axis runs over, the one named last changes fastest.
Arguments:
- tokens: bfloat16 [4, 64, 4096], P('weight', ('groups', 'dp')), parts along dimension 1, may hold values from -6 to 6
- gate_blocks: bfloat16 [1792, 128, 128], P('weight'), may hold values from -0.125 to 0.125
- up_blocks: bfloat16 [1792, 128, 128], P('weight'), may hold values from -0.125 to 0.125
- down_blocks: bfloat16 [1792, 128, 128], P('weight'), may hold values from -0.0625 to 0.0625
- row_starts: int32 [113], replicated, may hold values from 0 to 1792, as said below
- gate_cols: int32 [1792], P('weight'), may hold values from 0 to 31, as said below
- down_cols: int32 [1792], P('weight'), may hold values from 0 to 31, as said below
Outputs:
- mixed_out: bfloat16 [4, 64, 4096], P(None, ('groups', 'dp'), 'weight'), parts along dimension 1
The draws below stay inside these ranges and needn't reach their ends.
There are 2 independent parts, one for each index of `groups`. The reference program is written for one: setup_inputs(seed, part) draws one part's arguments, and reference() takes and returns one part's arrays. A program takes and returns all parts, laid end to end along the dimension named above; an argument that names none is the same for every part. Nothing has to cross between parts.
Inputs may be any that keep to these rules, and one draw needn't show every extreme that they name: row_starts[0] = 0 and row_starts[112] = 1792; each row of blocks f holds row_starts[f+1] - row_starts[f] blocks, from 8 to 24, both reached; the down projection's rows of blocks hold the same counts as the gate's. `gate_cols`: within a row of blocks the entries rise strictly. `down_cols`: within a row of blocks (given by row_starts) the entries rise strictly.
All inputs are finite; a program needn't handle non-finite values.
Results may differ from the reference program's by a relative error of at most 0.017.
Values may be sent and summed in bfloat16 or wider, within the bound.
No kernel may reach another device: no remote copies, remote signals or barrier semaphores. Data moves between devices by JAX's collectives and lax.ppermute only.
A program may use at most 128 MiB of HBM per device.

```python
import math
import jax
import jax.numpy as jnp
from jax import lax

D = 4096
FF = 14336
BLK = 128
SLAB = 32
DB = 32
FB = 112
NNZ = 1792
N_WEIGHT = 4


def row_counts(key):
    pair_count = FB // 2
    max_shift = DB // 4
    shifts = jax.random.randint(jax.random.fold_in(key, 11), (pair_count,), -max_shift, max_shift + 1).astype(jnp.int32)
    shifts = shifts.at[0].set(max_shift)
    row_shift = jnp.concatenate([shifts, -shifts])
    shuffled = jax.random.permutation(jax.random.fold_in(key, 12), FB).astype(jnp.int32)
    return jnp.zeros((FB,), jnp.int32).at[shuffled].set(DB // 2 + row_shift)


def pick_columns(key, counts):
    row_keys = jax.random.split(key, FB)
    shuffles = jax.vmap(lambda row_key: jax.random.permutation(row_key, DB))(row_keys).astype(jnp.int32)
    position = jnp.argsort(shuffles, axis=1, stable=True).astype(jnp.int32)
    chosen = position < counts[:, None]
    flat_index = jnp.arange(FB * DB, dtype=jnp.int32).reshape(FB, DB)
    sort_key = jnp.where(chosen, flat_index, flat_index + FB * DB).reshape(-1)
    sorted_idx = jnp.argsort(sort_key, stable=True)[:NNZ].astype(jnp.int32)
    return (sorted_idx % DB).astype(jnp.int32)


def draw_row_starts(key, part):
    counts = row_counts(key)
    return jnp.concatenate([jnp.zeros((1,), jnp.int32), jnp.cumsum(counts).astype(jnp.int32)]).astype(jnp.int32)


def draw_gate_cols(key, part):
    counts = row_counts(key)
    key = jax.random.fold_in(key, 21)
    return pick_columns(key, counts)


def draw_down_cols(key, part):
    counts = row_counts(key)
    key = jax.random.fold_in(key, 31)
    return pick_columns(key, counts)


def block_levels(rng, shape, cuts, least, high):
    def one(dim, blocks):
        heights = jax.random.uniform(jax.random.fold_in(jax.random.fold_in(rng, 6), dim), (blocks,), jnp.float32, least / len(cuts), high / len(cuts))
        return jnp.repeat(jnp.exp(heights), shape[dim] // blocks).reshape((-1,) + (1,) * (len(shape) - dim - 1))

    level = one(*cuts[0])
    for cut in cuts[1:]:
        level = level * one(*cut)
    return level


def bell_draw(rng, shape, scale, most, cuts=(), kind=jnp.bfloat16):
    factor_of = block_levels(rng, shape, cuts, -0.22, 0.18) if cuts else 1.0
    entries = jax.random.normal(rng, shape, jnp.float32) * scale * factor_of
    return jnp.minimum(jnp.maximum(entries, -most), most).astype(kind)


def setup_inputs(seed: int = 0, part: int = 0) -> dict:
    key_of = jax.random.split(jax.random.key(seed), 8)
    part_keys = jax.random.split(jax.random.fold_in(key_of[7], part), 8)
    return {
        "tokens": bell_draw(part_keys[0], (N_WEIGHT, SLAB, D), 1.0, 6.0, ((0, 4), (1, 4))),
        "gate_blocks": bell_draw(key_of[1], (NNZ, BLK, BLK), (D // 2) ** -0.5, 0.125, ((0, 4),)),
        "up_blocks": bell_draw(key_of[2], (NNZ, BLK, BLK), (D // 2) ** -0.5, 0.125, ((0, 4),)),
        "down_blocks": bell_draw(key_of[3], (NNZ, BLK, BLK), (FF // 2) ** -0.5, 0.0625, ((0, 4),)),
        "row_starts": draw_row_starts(jax.random.fold_in(key_of[7], 71), part),
        "gate_cols": draw_gate_cols(jax.random.fold_in(key_of[7], 71), part),
        "down_cols": draw_down_cols(jax.random.fold_in(key_of[7], 71), part),
    }


HIGHEST_PRECISION = lax.Precision.HIGHEST


def block_rows(row_starts):
    block_index = jnp.arange(NNZ, dtype=jnp.int32)
    return jnp.sum((row_starts[1:][None, :] <= block_index[:, None]).astype(jnp.int32), axis=1).astype(jnp.int32)


def reference(tokens, gate_blocks, up_blocks, down_blocks, row_starts, gate_cols, down_cols):
    row_data = tokens.reshape(-1, D)
    token_count = row_data.shape[0]
    by_column = row_data.reshape(token_count, DB, BLK).transpose(1, 0, 2)
    block_owner = block_rows(row_starts)
    group_size = math.gcd(NNZ, 16)
    step_count = NNZ // group_size

    def regroup(values):
        return values.reshape((step_count, group_size) + values.shape[1:])

    def up_step(totals, pieces):
        gate_acc, up_acc = totals
        gate_piece, up_piece, col_ids, row_ids = pieces
        picked = by_column[col_ids].astype(jnp.float32)
        gate_term = jnp.einsum("irk,ikj->irj", picked, gate_piece.astype(jnp.float32), precision=HIGHEST_PRECISION)
        up_term = jnp.einsum("irk,ikj->irj", picked, up_piece.astype(jnp.float32), precision=HIGHEST_PRECISION)
        return (gate_acc.at[row_ids].add(gate_term), up_acc.at[row_ids].add(up_term)), None

    blank_rows = jnp.zeros((FB, token_count, BLK), jnp.float32)
    (gate_acc, up_acc), _ = lax.scan(
        up_step, (blank_rows, blank_rows),
        (regroup(gate_blocks), regroup(up_blocks), regroup(gate_cols), regroup(block_owner)))
    hidden = (jax.nn.silu(gate_acc) * up_acc).astype(jnp.bfloat16)

    def down_step(result_acc, pieces):
        down_piece, col_ids, row_ids = pieces
        source = hidden[row_ids].astype(jnp.float32)
        block_term = jnp.einsum("irk,ikj->irj", source, down_piece.astype(jnp.float32), precision=HIGHEST_PRECISION)
        return result_acc.at[col_ids].add(block_term), None

    result_acc, _ = lax.scan(
        down_step, jnp.zeros((DB, token_count, BLK), jnp.float32),
        (regroup(down_blocks), regroup(down_cols), regroup(block_owner)))
    mixed_out = result_acc.transpose(1, 0, 2).reshape(token_count, D).astype(jnp.bfloat16)
    return mixed_out.reshape(N_WEIGHT, SLAB, D)
```

```python
import functools

import jax
import jax.numpy as jnp
from jax import lax
from jax.experimental import pallas as pl
from jax.experimental.pallas import tpu as pltpu
from jax.sharding import PartitionSpec as P

GROUP = 8
EDGE = 24
VM = pl.BlockSpec(memory_space=pltpu.VMEM)
SM = pl.BlockSpec(memory_space=pltpu.SMEM)
HB = pl.BlockSpec(memory_space=pltpu.HBM)
F32 = jnp.float32
BF16 = jnp.bfloat16


def limit(mib):
    return pltpu.CompilerParams(vmem_limit_bytes=mib * 2**20)


def cost(flops):
    return pl.CostEstimate(flops=flops, bytes_accessed=2**20, transcendentals=0)


def largest_unroll(steps, most):
    return max(u for u in range(1, most + 1) if steps % u == 0)


def in_vmem(value):
    return pltpu.with_memory_space_constraint(value, pltpu.VMEM)


def in_hbm(value):
    return pltpu.with_memory_space_constraint(value, pltpu.HBM)


def prepare_kernel(starts, gate, up, slots, edge_gate, edge_up, sems, *, count):
    copies = []
    for k, (source, target) in enumerate(((gate, edge_gate), (up, edge_up))):
        for side, first in enumerate((0, count - EDGE)):
            copies.append(
                pltpu.make_async_copy(source.at[pl.ds(first, EDGE)], target.at[side], sems.at[k, side])
            )
    for copy in copies:
        copy.start()
    first_block = lax.axis_index("weight") * count
    lanes = lax.broadcasted_iota(jnp.int32, slots.shape, 1)
    place = first_block + lax.broadcasted_iota(jnp.int32, slots.shape, 0) * 128 + lanes
    row = jnp.zeros(slots.shape, jnp.int32)
    first_row, enters, leaves = 0, 1, 1
    for f in range(1, starts.shape[0]):
        start = starts[f]
        row += (start <= place).astype(jnp.int32)
        first_row += (start <= first_block).astype(jnp.int32)
        enters = jnp.where(start == first_block, 0, enters)
        leaves = jnp.where(start == first_block + count, 0, leaves)
    enters = jnp.where(first_block == 0, 0, enters)
    flag_row = lax.broadcasted_iota(jnp.int32, slots.shape, 0) == slots.shape[0] - 1
    slots[...] = jnp.where(flag_row, jnp.where(lanes == 0, enters, leaves), row - first_row)
    for copy in copies:
        copy.wait()


def slot_of(slots, block):
    if isinstance(block, int):
        return slots[block // 128, block % 128]
    return slots[lax.shift_right_logical(block, 7), lax.bitwise_and(block, 127)]


def edge_kernel(slots, cols, *refs):
    pieces, (edge_gate, edge_up, by_col, to_prev, to_next, whole) = refs[:-6], refs[-6:]
    size = len(pieces)
    count = cols.shape[0]
    col_blocks, rows = by_col.shape[0] - 1, by_col.shape[1]
    me = lax.axis_index("weight")
    for step, piece in enumerate(pieces):
        whole[lax.rem(me + size - step, size)] = piece[0]
    merged = whole[...].reshape(rows, col_blocks * 128)
    for c in range(col_blocks):
        by_col[c] = merged[:, c * 128 : (c + 1) * 128]
    by_col[col_blocks] = jnp.zeros((rows, 128), BF16)
    last_flag = slots.shape[0] - 1
    for side, first, sent in ((0, 0, to_prev), (1, count - EDGE, to_next)):
        mine = slot_of(slots, 0 if side == 0 else count - 1)
        picked = []
        for q in range(EDGE):
            block = first + q
            picked.append(by_col[jnp.where(slot_of(slots, block) == mine, cols[block], col_blocks)])
        weights = jnp.concatenate(
            [edge_gate[side].reshape(EDGE * 128, 128), edge_up[side].reshape(EDGE * 128, 128)], axis=1
        )
        total = jnp.dot(jnp.concatenate(picked, axis=1), weights, preferred_element_type=F32)
        sent[...] = jnp.where(slots[last_flag, side] == 1, total, 0.0).astype(BF16)


def silu_gate(sums):
    gate, up = sums[..., :128], sums[..., 128:]
    return (gate / (1 + jnp.exp(-gate)) * up).astype(BF16)


def hidden_kernel(slots, cols, by_col, gate, up, hidden, edges, sums, *, unroll):
    col_blocks, rows = by_col.shape[0] - 1, by_col.shape[1]
    count = cols.shape[0]
    sums[...] = jnp.zeros_like(sums)

    def step(it, carry):
        for j in range(unroll):
            first = (it * unroll + j) * GROUP
            slot = slot_of(slots, first)
            even, odd = [], []
            for q in range(GROUP):
                col, is_odd = cols[first + q], (slot_of(slots, first + q) & 1) == 1
                even.append(by_col[jnp.where(is_odd, col_blocks, col)])
                odd.append(by_col[jnp.where(is_odd, col, col_blocks)])
            left = jnp.concatenate([jnp.concatenate(even, axis=1), jnp.concatenate(odd, axis=1)], axis=0)
            right = jnp.concatenate(
                [ref[pl.ds(first, GROUP)].reshape(GROUP * 128, 128) for ref in (gate, up)], axis=1
            )
            part = jnp.dot(left, right, preferred_element_type=F32)
            at_even, at_odd = slot + (slot & 1), slot | 1
            old_even, old_odd = sums[at_even], sums[at_odd]
            sums[at_even] = old_even + part[:rows]
            sums[at_odd] = old_odd + part[rows:]
        return carry

    lax.fori_loop(0, count // GROUP // unroll, step, 0)
    hidden[...] = silu_gate(sums[...])
    edges[0] = sums[0]
    edges[1] = sums[slot_of(slots, count - 1)]


def down_kernel(slots, cols, hidden, edges, from_prev, from_next, down, *refs, unroll):
    outs, (rows_in, sums) = refs[:-2], refs[-2:]
    size = len(outs)
    count = cols.shape[0]
    rows = hidden.shape[1]
    col_blocks = sums.shape[1]
    rows_in[...] = hidden[...]
    rows_in[0] = silu_gate(edges[0] + from_prev[...].astype(F32))
    rows_in[slot_of(slots, count - 1)] = silu_gate(edges[1] + from_next[...].astype(F32))
    sums[...] = jnp.zeros_like(sums)

    def step(it, carry):
        for j in range(unroll):
            first = (it * unroll + j) * GROUP
            slot = slot_of(slots, first)
            left = jnp.concatenate([rows_in[slot + (slot & 1)], rows_in[slot | 1]], axis=0)
            right = jnp.concatenate([down[first + q] for q in range(GROUP)], axis=1)
            part = jnp.dot(left, right, preferred_element_type=F32)
            for half in range(0, GROUP, 4):
                at = [(slot_of(slots, first + q) & 1, cols[first + q]) for q in range(half, half + 4)]
                old = [sums[odd, col] for odd, col in at]
                for q, (odd, col) in enumerate(at):
                    term = part[:, (half + q) * 128 : (half + q + 1) * 128]
                    sums[odd, col] = old[q] + jnp.where(odd == 1, term[rows:], term[:rows])
        return carry

    lax.fori_loop(0, count // GROUP // unroll, step, 0)
    me = lax.axis_index("weight")
    share = col_blocks // size
    for distance, out in enumerate(outs):
        first = lax.rem(me + distance, size) * share
        for c in range(share):
            total = sums[0, first + c] + sums[1, first + c]
            out[:, c * 128 : (c + 1) * 128] = total.astype(out.dtype)


def per_device(tokens, gate_blocks, up_blocks, down_blocks, row_starts, gate_cols, down_cols):
    count, width, _ = gate_blocks.shape
    model_width = tokens.shape[2]
    col_blocks = model_width // width
    size = lax.axis_size("weight")
    slab = tokens.shape[1]
    rows = size * slab
    row_slots = (count - 1) // GROUP + 3

    def shift(value, distance):
        return lax.ppermute(value, "weight", [(d, (d + distance) % size) for d in range(size)])

    pieces = [tokens] + [shift(tokens, distance) for distance in range(1, size)]
    slot_rows = -(-count // 128) + 1
    slots, edge_gate, edge_up = pl.pallas_call(
        functools.partial(prepare_kernel, count=count),
        out_shape=(
            jax.ShapeDtypeStruct((slot_rows, 128), jnp.int32),
            pltpu.VMEM((2, EDGE, width, width), BF16),
            pltpu.VMEM((2, EDGE, width, width), BF16),
        ),
        in_specs=[SM, HB, HB],
        out_specs=(VM, VM, VM),
        scratch_shapes=[pltpu.SemaphoreType.DMA((2, 2))],
        compiler_params=limit(4),
        cost_estimate=cost(2**36),
        name="prepare",
    )(row_starts, in_hbm(gate_blocks), in_hbm(up_blocks))
    by_col, to_prev, to_next = pl.pallas_call(
        edge_kernel,
        out_shape=(
            pltpu.VMEM((col_blocks + 1, rows, width), BF16),
            jax.ShapeDtypeStruct((rows, 2 * width), BF16),
            jax.ShapeDtypeStruct((rows, 2 * width), BF16),
        ),
        in_specs=[SM, SM] + [VM] * (size + 2),
        out_specs=(VM, VM, VM),
        scratch_shapes=[pltpu.VMEM((size, slab, model_width), BF16)],
        compiler_params=limit(4),
        name="edges",
    )(slots, gate_cols, *pieces, edge_gate, edge_up)
    from_next = lax.ppermute(to_prev, "weight", [(d + 1, d) for d in range(size - 1)])
    from_prev = lax.ppermute(to_next, "weight", [(d, d + 1) for d in range(size - 1)])
    hidden, edges = pl.pallas_call(
        functools.partial(hidden_kernel, unroll=largest_unroll(count // GROUP, 28)),
        out_shape=(
            pltpu.VMEM((row_slots, rows, width), BF16),
            pltpu.VMEM((2, rows, 2 * width), F32),
        ),
        in_specs=[SM, SM, VM, VM, VM],
        out_specs=(VM, VM),
        scratch_shapes=[pltpu.VMEM((row_slots, rows, 2 * width), F32)],
        compiler_params=limit(8),
        cost_estimate=cost(2**30),
        name="hidden",
    )(slots, gate_cols, by_col, in_vmem(gate_blocks), in_vmem(up_blocks))
    outs = pl.pallas_call(
        functools.partial(down_kernel, unroll=largest_unroll(count // GROUP, 28)),
        out_shape=tuple(
            jax.ShapeDtypeStruct((rows, model_width // size), BF16 if distance else F32)
            for distance in range(size)
        ),
        in_specs=[SM, SM] + [VM] * 5,
        out_specs=(VM,) * size,
        scratch_shapes=[
            pltpu.VMEM((row_slots, rows, width), BF16),
            pltpu.VMEM((2, col_blocks, rows, width), F32),
        ],
        compiler_params=limit(8),
        name="down",
    )(slots, down_cols, hidden, edges, from_prev, from_next, in_vmem(down_blocks))
    total = outs[0]
    for distance in range(1, size):
        total = total + shift(outs[distance], distance).astype(F32)
    return total.astype(BF16).reshape(size, slab, model_width // size)


def solution(mesh):
    in_specs = (
        P("weight", ("groups", "dp"), None),
        P("weight", None, None),
        P("weight", None, None),
        P("weight", None, None),
        P(),
        P("weight"),
        P("weight"),
    )
    out_specs = P(None, ("groups", "dp"), "weight")
    return jax.shard_map(
        per_device, mesh=mesh, in_specs=in_specs, out_specs=out_specs, check_vma=False
    )
```

```python
import functools

import jax
import jax.numpy as jnp
from jax import lax
from jax.experimental import pallas as pl
from jax.experimental.pallas import tpu as pltpu
from jax.sharding import PartitionSpec as P

GROUP = 8
EDGE = 24
VM = pl.BlockSpec(memory_space=pltpu.VMEM)
SM = pl.BlockSpec(memory_space=pltpu.SMEM)
HB = pl.BlockSpec(memory_space=pltpu.HBM)
F32 = jnp.float32
BF16 = jnp.bfloat16


def limit(mib):
    return pltpu.CompilerParams(vmem_limit_bytes=mib * 2**20)


def cost(flops):
    return pl.CostEstimate(flops=flops, bytes_accessed=2**20, transcendentals=0)


def largest_unroll(steps, most):
    return max(u for u in range(1, most + 1) if steps % u == 0)


def in_vmem(value):
    return pltpu.with_memory_space_constraint(value, pltpu.VMEM)


def in_hbm(value):
    return pltpu.with_memory_space_constraint(value, pltpu.HBM)


def prepare_kernel(starts, gate, up, slots, edge_gate, edge_up, sems, *, count):
    copies = []
    for k, (source, target) in enumerate(((gate, edge_gate), (up, edge_up))):
        for side, first in enumerate((0, count - EDGE)):
            copies.append(
                pltpu.make_async_copy(source.at[pl.ds(first, EDGE)], target.at[side], sems.at[k, side])
            )
    for copy in copies:
        copy.start()
    first_block = lax.axis_index("weight") * count
    lanes = lax.broadcasted_iota(jnp.int32, slots.shape, 1)
    place = first_block + lax.broadcasted_iota(jnp.int32, slots.shape, 0) * 128 + lanes
    row = jnp.zeros(slots.shape, jnp.int32)
    first_row, enters, leaves = 0, 1, 1
    for f in range(1, starts.shape[0]):
        start = starts[f]
        row += (start <= place).astype(jnp.int32)
        first_row += (start <= first_block).astype(jnp.int32)
        enters = jnp.where(start == first_block, 0, enters)
        leaves = jnp.where(start == first_block + count, 0, leaves)
    enters = jnp.where(first_block == 0, 0, enters)
    flag_row = lax.broadcasted_iota(jnp.int32, slots.shape, 0) == slots.shape[0] - 1
    slots[...] = jnp.where(flag_row, jnp.where(lanes == 0, enters, leaves), row - first_row)
    for copy in copies:
        copy.wait()


def slot_of(slots, block):
    if isinstance(block, int):
        return slots[block // 128, block % 128]
    return slots[lax.shift_right_logical(block, 7), lax.bitwise_and(block, 127)]


def edge_kernel(slots, cols, *refs):
    pieces, (edge_gate, edge_up, by_col, to_inner, to_outer, whole) = refs[:-6], refs[-6:]
    size = len(pieces)
    count = cols.shape[0]
    col_blocks, rows = by_col.shape[0] - 1, by_col.shape[1]
    me = lax.axis_index("weight")
    for distance, piece in enumerate(pieces):
        whole[lax.bitwise_xor(me, distance)] = piece[0]
    merged = whole[...].reshape(rows, col_blocks * 128)
    for c in range(col_blocks):
        by_col[c] = merged[:, c * 128 : (c + 1) * 128]
    by_col[col_blocks] = jnp.zeros((rows, 128), BF16)
    last_flag = slots.shape[0] - 1
    is_odd = (me & 1) == 1
    parts = []
    for side, first in ((0, 0), (1, count - EDGE)):
        mine = slot_of(slots, 0 if side == 0 else count - 1)
        picked = []
        for q in range(EDGE):
            block = first + q
            picked.append(by_col[jnp.where(slot_of(slots, block) == mine, cols[block], col_blocks)])
        weights = jnp.concatenate(
            [edge_gate[side].reshape(EDGE * 128, 128), edge_up[side].reshape(EDGE * 128, 128)], axis=1
        )
        total = jnp.dot(jnp.concatenate(picked, axis=1), weights, preferred_element_type=F32)
        parts.append(jnp.where(slots[last_flag, side] == 1, total, 0.0).astype(BF16))
    to_inner[...] = jnp.where(is_odd, parts[0], parts[1])
    to_outer[...] = jnp.where(is_odd, parts[1], parts[0])


def silu_gate(sums):
    gate, up = sums[..., :128], sums[..., 128:]
    return (gate / (1 + jnp.exp(-gate)) * up).astype(BF16)


def hidden_kernel(slots, cols, by_col, gate, up, hidden, edges, sums, *, unroll):
    col_blocks, rows = by_col.shape[0] - 1, by_col.shape[1]
    count = cols.shape[0]
    sums[...] = jnp.zeros_like(sums)

    def step(it, carry):
        for j in range(unroll):
            first = (it * unroll + j) * GROUP
            slot = slot_of(slots, first)
            even, odd = [], []
            for q in range(GROUP):
                col, is_odd = cols[first + q], (slot_of(slots, first + q) & 1) == 1
                even.append(by_col[jnp.where(is_odd, col_blocks, col)])
                odd.append(by_col[jnp.where(is_odd, col, col_blocks)])
            left = jnp.concatenate([jnp.concatenate(even, axis=1), jnp.concatenate(odd, axis=1)], axis=0)
            right = jnp.concatenate(
                [ref[pl.ds(first, GROUP)].reshape(GROUP * 128, 128) for ref in (gate, up)], axis=1
            )
            part = jnp.dot(left, right, preferred_element_type=F32)
            at_even, at_odd = slot + (slot & 1), slot | 1
            old_even, old_odd = sums[at_even], sums[at_odd]
            sums[at_even] = old_even + part[:rows]
            sums[at_odd] = old_odd + part[rows:]
        return carry

    lax.fori_loop(0, count // GROUP // unroll, step, 0)
    hidden[...] = silu_gate(sums[...])
    edges[0] = sums[0]
    edges[1] = sums[slot_of(slots, count - 1)]


def down_kernel(slots, cols, hidden, edges, from_inner, from_outer, down, *refs, unroll):
    outs, (rows_in, sums) = refs[:-2], refs[-2:]
    size = len(outs)
    count = cols.shape[0]
    rows = hidden.shape[1]
    col_blocks = sums.shape[1]
    rows_in[...] = hidden[...]
    me = lax.axis_index("weight")
    is_odd = (me & 1) == 1
    inner, outer = from_inner[...].astype(F32), from_outer[...].astype(F32)
    rows_in[0] = silu_gate(edges[0] + jnp.where(is_odd, inner, outer))
    rows_in[slot_of(slots, count - 1)] = silu_gate(edges[1] + jnp.where(is_odd, outer, inner))
    sums[...] = jnp.zeros_like(sums)

    def step(it, carry):
        for j in range(unroll):
            first = (it * unroll + j) * GROUP
            slot = slot_of(slots, first)
            left = jnp.concatenate([rows_in[slot + (slot & 1)], rows_in[slot | 1]], axis=0)
            right = jnp.concatenate([down[first + q] for q in range(GROUP)], axis=1)
            part = jnp.dot(left, right, preferred_element_type=F32)
            for half in range(0, GROUP, 4):
                at = [(slot_of(slots, first + q) & 1, cols[first + q]) for q in range(half, half + 4)]
                old = [sums[odd, col] for odd, col in at]
                for q, (odd, col) in enumerate(at):
                    term = part[:, (half + q) * 128 : (half + q + 1) * 128]
                    sums[odd, col] = old[q] + jnp.where(odd == 1, term[rows:], term[:rows])
        return carry

    lax.fori_loop(0, count // GROUP // unroll, step, 0)
    share = col_blocks // size
    for distance, out in enumerate(outs):
        first = lax.bitwise_xor(me, distance) * share
        for c in range(share):
            total = sums[0, first + c] + sums[1, first + c]
            out[:, c * 128 : (c + 1) * 128] = total.astype(out.dtype)


def per_device(tokens, gate_blocks, up_blocks, down_blocks, row_starts, gate_cols, down_cols):
    count, width, _ = gate_blocks.shape
    model_width = tokens.shape[2]
    col_blocks = model_width // width
    size = lax.axis_size("weight")
    slab = tokens.shape[1]
    rows = size * slab
    row_slots = (count - 1) // GROUP + 3

    def swap(value, distance):
        return lax.ppermute(value, "weight", [(d, d ^ distance) for d in range(size)])

    order = list(range(2, size)) + [1]
    arrived = {distance: swap(tokens, distance) for distance in order}
    pieces = [tokens] + [arrived[distance] for distance in range(1, size)]
    slot_rows = -(-count // 128) + 1
    slots, edge_gate, edge_up = pl.pallas_call(
        functools.partial(prepare_kernel, count=count),
        out_shape=(
            jax.ShapeDtypeStruct((slot_rows, 128), jnp.int32),
            pltpu.VMEM((2, EDGE, width, width), BF16),
            pltpu.VMEM((2, EDGE, width, width), BF16),
        ),
        in_specs=[SM, HB, HB],
        out_specs=(VM, VM, VM),
        scratch_shapes=[pltpu.SemaphoreType.DMA((2, 2))],
        compiler_params=limit(4),
        cost_estimate=cost(2**36),
        name="prepare",
    )(row_starts, in_hbm(gate_blocks), in_hbm(up_blocks))
    by_col, to_inner, to_outer = pl.pallas_call(
        edge_kernel,
        out_shape=(
            pltpu.VMEM((col_blocks + 1, rows, width), BF16),
            jax.ShapeDtypeStruct((rows, 2 * width), BF16),
            jax.ShapeDtypeStruct((rows, 2 * width), BF16),
        ),
        in_specs=[SM, SM] + [VM] * (size + 2),
        out_specs=(VM, VM, VM),
        scratch_shapes=[pltpu.VMEM((size, slab, model_width), BF16)],
        compiler_params=limit(4),
        name="edges",
    )(slots, gate_cols, *pieces, edge_gate, edge_up)
    outer_pairs = [(d, (d + 1 if d % 2 else d - 1) % size) for d in range(size)]
    from_outer = lax.ppermute(to_outer, "weight", outer_pairs)
    from_inner = swap(to_inner, 1)
    hidden, edges = pl.pallas_call(
        functools.partial(hidden_kernel, unroll=largest_unroll(count // GROUP, 28)),
        out_shape=(
            pltpu.VMEM((row_slots, rows, width), BF16),
            pltpu.VMEM((2, rows, 2 * width), F32),
        ),
        in_specs=[SM, SM, VM, VM, VM],
        out_specs=(VM, VM),
        scratch_shapes=[pltpu.VMEM((row_slots, rows, 2 * width), F32)],
        compiler_params=limit(8),
        cost_estimate=cost(2**30),
        name="hidden",
    )(slots, gate_cols, by_col, in_vmem(gate_blocks), in_vmem(up_blocks))
    outs = pl.pallas_call(
        functools.partial(down_kernel, unroll=largest_unroll(count // GROUP, 28)),
        out_shape=tuple(
            jax.ShapeDtypeStruct((rows, model_width // size), BF16 if distance else F32)
            for distance in range(size)
        ),
        in_specs=[SM, SM] + [VM] * 5,
        out_specs=(VM,) * size,
        scratch_shapes=[
            pltpu.VMEM((row_slots, rows, width), BF16),
            pltpu.VMEM((2, col_blocks, rows, width), F32),
        ],
        compiler_params=limit(8),
        name="down",
    )(slots, down_cols, hidden, edges, from_inner, from_outer, in_vmem(down_blocks))
    received = {distance: swap(outs[distance], distance) for distance in order}
    total = outs[0]
    for distance in order:
        total = total + received[distance].astype(F32)
    return total.astype(BF16).reshape(size, slab, model_width // size)


def solution(mesh):
    in_specs = (
        P("weight", ("groups", "dp"), None),
        P("weight", None, None),
        P("weight", None, None),
        P("weight", None, None),
        P(),
        P("weight"),
        P("weight"),
    )
    out_specs = P(None, ("groups", "dp"), "weight")
    return jax.shard_map(
        per_device, mesh=mesh, in_specs=in_specs, out_specs=out_specs, check_vma=False
    )
```

```python
import functools

import jax
import jax.numpy as jnp
from jax import lax
from jax.experimental import pallas as pl
from jax.experimental.pallas import tpu as pltpu
from jax.sharding import PartitionSpec as P

GROUP = 8
EDGE = 24
VM = pl.BlockSpec(memory_space=pltpu.VMEM)
SM = pl.BlockSpec(memory_space=pltpu.SMEM)
HB = pl.BlockSpec(memory_space=pltpu.HBM)
F32 = jnp.float32
BF16 = jnp.bfloat16


def limit(mib):
    return pltpu.CompilerParams(vmem_limit_bytes=mib * 2**20)


def cost(flops):
    return pl.CostEstimate(flops=flops, bytes_accessed=2**10, transcendentals=0)


def largest_divisor(steps, most):
    return max(u for u in range(1, most + 1) if steps % u == 0)


def in_vmem(value):
    return pltpu.with_memory_space_constraint(value, pltpu.VMEM)


def in_hbm(value):
    return pltpu.with_memory_space_constraint(value, pltpu.HBM)


def prepare_kernel(starts, up, slots, edge_up, smem_starts, sems, *, count):
    copies = [pltpu.make_async_copy(starts, smem_starts, sems.at[2])]
    for side, first in enumerate((0, count - EDGE)):
        copies.append(pltpu.make_async_copy(up.at[pl.ds(first, EDGE)], edge_up.at[side], sems.at[side]))
    for copy in copies:
        copy.start()
    first_block = lax.axis_index("weight") * count
    lanes = lax.broadcasted_iota(jnp.int32, slots.shape, 1)
    place = first_block + lax.broadcasted_iota(jnp.int32, slots.shape, 0) * 128 + lanes
    row = jnp.zeros(slots.shape, jnp.int32)
    first_row, enters, leaves = 0, 1, 1
    copies[0].wait()
    for f in range(1, smem_starts.shape[0]):
        start = smem_starts[f]
        row += (start <= place).astype(jnp.int32)
        first_row += (start <= first_block).astype(jnp.int32)
        enters = jnp.where(start == first_block, 0, enters)
        leaves = jnp.where(start == first_block + count, 0, leaves)
    enters = jnp.where(first_block == 0, 0, enters)
    flag_row = lax.broadcasted_iota(jnp.int32, slots.shape, 0) == slots.shape[0] - 1
    slots[...] = jnp.where(flag_row, jnp.where(lanes == 0, enters, leaves), row - first_row)
    for copy in copies[1:]:
        copy.wait()


def slot_of(slots, block):
    if isinstance(block, int):
        return slots[block // 128, block % 128]
    return slots[lax.shift_right_logical(block, 7), lax.bitwise_and(block, 127)]


def edge_kernel(slots, cols, *refs):
    pieces, (gate, edge_up, by_col, to_inner, to_outer, whole) = refs[:-6], refs[-6:]
    size = len(pieces)
    count = cols.shape[0]
    col_blocks, rows = by_col.shape[0] - 1, by_col.shape[1]
    me = lax.axis_index("weight")
    for distance, piece in enumerate(pieces):
        whole[lax.bitwise_xor(me, distance)] = piece[0]
    merged = whole[...].reshape(rows, col_blocks * 128)
    for c in range(col_blocks):
        by_col[c] = merged[:, c * 128 : (c + 1) * 128]
    by_col[col_blocks] = jnp.zeros((rows, 128), BF16)
    last_flag = slots.shape[0] - 1
    is_odd = (me & 1) == 1
    parts = []
    for side, first in ((0, 0), (1, count - EDGE)):
        mine = slot_of(slots, 0 if side == 0 else count - 1)
        picked = []
        for q in range(EDGE):
            block = first + q
            picked.append(by_col[jnp.where(slot_of(slots, block) == mine, cols[block], col_blocks)])
        weights = jnp.concatenate(
            [gate[first : first + EDGE].reshape(EDGE * 128, 128), edge_up[side].reshape(EDGE * 128, 128)], axis=1
        )
        total = jnp.dot(jnp.concatenate(picked, axis=1), weights, preferred_element_type=F32)
        parts.append(jnp.where(slots[last_flag, side] == 1, total, 0.0).astype(BF16))
    to_inner[...] = jnp.where(is_odd, parts[0], parts[1])
    to_outer[...] = jnp.where(is_odd, parts[1], parts[0])


def silu_gate(gate, up):
    return (gate / (1 + jnp.exp(-gate)) * up).astype(BF16)


def add_rows(slots, cols, by_col, weights, sums, unroll):
    col_blocks, rows = by_col.shape[0] - 1, by_col.shape[1]
    count = cols.shape[0]
    sums[...] = jnp.zeros_like(sums)

    def step(it, carry):
        for j in range(unroll):
            first = (it * unroll + j) * GROUP
            slot = slot_of(slots, first)
            even, odd = [], []
            for q in range(GROUP):
                col, is_odd = cols[first + q], (slot_of(slots, first + q) & 1) == 1
                even.append(by_col[jnp.where(is_odd, col_blocks, col)])
                odd.append(by_col[jnp.where(is_odd, col, col_blocks)])
            left = jnp.concatenate([jnp.concatenate(even, axis=1), jnp.concatenate(odd, axis=1)], axis=0)
            right = weights[pl.ds(first, GROUP)].reshape(GROUP * 128, 128)
            part = jnp.dot(left, right, preferred_element_type=F32)
            at_even, at_odd = slot + (slot & 1), slot | 1
            old_even, old_odd = sums[at_even], sums[at_odd]
            sums[at_even] = old_even + part[:rows]
            sums[at_odd] = old_odd + part[rows:]
        return carry

    lax.fori_loop(0, count // GROUP // unroll, step, 0)


def gate_kernel(slots, cols, by_col, gate, sums, *, unroll):
    add_rows(slots, cols, by_col, gate, sums, unroll)


def up_kernel(slots, cols, by_col, up, gate_sums, hidden, edges, sums, *, unroll):
    add_rows(slots, cols, by_col, up, sums, unroll)
    hidden[...] = silu_gate(gate_sums[...], sums[...])
    for side, slot in enumerate((0, slot_of(slots, cols.shape[0] - 1))):
        edges[side, 0] = gate_sums[slot]
        edges[side, 1] = sums[slot]


def down_kernel(slots, cols, hidden, edges, from_inner, from_outer, down, *refs, unroll):
    outs, (rows_in, sums) = refs[:-2], refs[-2:]
    size = len(outs)
    count = cols.shape[0]
    rows = hidden.shape[1]
    col_blocks = sums.shape[1]
    rows_in[...] = hidden[...]
    me = lax.axis_index("weight")
    is_odd = (me & 1) == 1
    inner, outer = from_inner[...].astype(F32), from_outer[...].astype(F32)
    before, after = jnp.where(is_odd, inner, outer), jnp.where(is_odd, outer, inner)
    for side, slot, part in ((0, 0, before), (1, slot_of(slots, count - 1), after)):
        rows_in[slot] = silu_gate(edges[side, 0] + part[:, :128], edges[side, 1] + part[:, 128:])
    sums[...] = jnp.zeros_like(sums)

    def step(it, carry):
        for j in range(unroll):
            first = (it * unroll + j) * GROUP
            slot = slot_of(slots, first)
            left = jnp.concatenate([rows_in[slot + (slot & 1)], rows_in[slot | 1]], axis=0)
            right = jnp.concatenate([down[first + q] for q in range(GROUP)], axis=1)
            part = jnp.dot(left, right, preferred_element_type=F32)
            for half in range(0, GROUP, 4):
                at = [(slot_of(slots, first + q) & 1, cols[first + q]) for q in range(half, half + 4)]
                old = [sums[odd, col] for odd, col in at]
                for q, (odd, col) in enumerate(at):
                    term = part[:, (half + q) * 128 : (half + q + 1) * 128]
                    sums[odd, col] = old[q] + jnp.where(odd == 1, term[rows:], term[:rows])
        return carry

    lax.fori_loop(0, count // GROUP // unroll, step, 0)
    share = col_blocks // size
    for distance, out in enumerate(outs):
        first = lax.bitwise_xor(me, distance) * share
        for c in range(share):
            total = sums[0, first + c] + sums[1, first + c]
            out[:, c * 128 : (c + 1) * 128] = total.astype(out.dtype)


def per_device(tokens, gate_blocks, up_blocks, down_blocks, row_starts, gate_cols, down_cols):
    count, width, _ = gate_blocks.shape
    model_width = tokens.shape[2]
    col_blocks = model_width // width
    size = lax.axis_size("weight")
    slab = tokens.shape[1]
    rows = size * slab
    row_slots = (count - 1) // GROUP + 3

    def swap(value, distance):
        return lax.ppermute(value, "weight", [(d, d ^ distance) for d in range(size)])

    order = list(range(2, size)) + [1]
    arrived = {distance: swap(tokens, distance) for distance in order}
    pieces = [tokens] + [arrived[distance] for distance in range(1, size)]
    slot_rows = -(-count // 128) + 1
    slots, edge_up = pl.pallas_call(
        functools.partial(prepare_kernel, count=count),
        out_shape=(
            jax.ShapeDtypeStruct((slot_rows, 128), jnp.int32),
            pltpu.VMEM((2, EDGE, width, width), BF16),
        ),
        in_specs=[HB, HB],
        out_specs=(VM, VM),
        scratch_shapes=[pltpu.SMEM(row_starts.shape, jnp.int32), pltpu.SemaphoreType.DMA((3,))],
        compiler_params=limit(4),
        cost_estimate=cost(2**36),
        name="prepare",
    )(in_hbm(row_starts), in_hbm(up_blocks))
    by_col, to_inner, to_outer = pl.pallas_call(
        edge_kernel,
        out_shape=(
            pltpu.VMEM((col_blocks + 1, rows, width), BF16),
            jax.ShapeDtypeStruct((rows, 2 * width), BF16),
            jax.ShapeDtypeStruct((rows, 2 * width), BF16),
        ),
        in_specs=[SM, SM] + [VM] * (size + 2),
        out_specs=(VM, VM, VM),
        scratch_shapes=[pltpu.VMEM((size, slab, model_width), BF16)],
        compiler_params=limit(4),
        cost_estimate=cost(2**19),
        name="edges",
    )(slots, gate_cols, *pieces, in_vmem(gate_blocks), edge_up)
    outer_pairs = [(d, (d + 1 if d % 2 else d - 1) % size) for d in range(size)]
    from_outer = lax.ppermute(to_outer, "weight", outer_pairs)
    from_inner = swap(to_inner, 1)
    unroll = largest_divisor(count // GROUP, 28)
    gate_sums = pl.pallas_call(
        functools.partial(gate_kernel, unroll=unroll),
        out_shape=pltpu.VMEM((row_slots, rows, width), F32),
        in_specs=[SM, SM, VM, VM],
        out_specs=VM,
        compiler_params=limit(8),
        cost_estimate=cost(2**20),
        name="gate",
    )(slots, gate_cols, by_col, in_vmem(gate_blocks))
    hidden, edges = pl.pallas_call(
        functools.partial(up_kernel, unroll=unroll),
        out_shape=(
            pltpu.VMEM((row_slots, rows, width), BF16),
            pltpu.VMEM((2, 2, rows, width), F32),
        ),
        in_specs=[SM, SM, VM, VM, VM],
        out_specs=(VM, VM),
        scratch_shapes=[pltpu.VMEM((row_slots, rows, width), F32)],
        compiler_params=limit(8),
        cost_estimate=cost(2**33),
        name="up",
    )(slots, gate_cols, by_col, in_vmem(up_blocks), in_vmem(gate_sums))
    outs = pl.pallas_call(
        functools.partial(down_kernel, unroll=unroll),
        out_shape=tuple(
            jax.ShapeDtypeStruct((rows, model_width // size), BF16 if distance else F32)
            for distance in range(size)
        ),
        in_specs=[SM, SM] + [VM] * 5,
        out_specs=(VM,) * size,
        scratch_shapes=[
            pltpu.VMEM((row_slots, rows, width), BF16),
            pltpu.VMEM((2, col_blocks, rows, width), F32),
        ],
        compiler_params=limit(8),
        cost_estimate=cost(2**18),
        name="down",
    )(slots, down_cols, hidden, edges, from_inner, from_outer, in_vmem(down_blocks))
    received = {distance: swap(outs[distance], distance) for distance in order}
    total = outs[0]
    for distance in order:
        total = total + received[distance].astype(F32)
    return total.astype(BF16).reshape(size, slab, model_width // size)


def solution(mesh):
    in_specs = (
        P("weight", ("groups", "dp"), None),
        P("weight", None, None),
        P("weight", None, None),
        P("weight", None, None),
        P(),
        P("weight"),
        P("weight"),
    )
    out_specs = P(None, ("groups", "dp"), "weight")
    return jax.shard_map(
        per_device, mesh=mesh, in_specs=in_specs, out_specs=out_specs, check_vma=False
    )
```

```python
import functools

import jax
import jax.numpy as jnp
from jax import lax
from jax.experimental import pallas as pl
from jax.experimental.pallas import tpu as pltpu
from jax.sharding import PartitionSpec as P

GROUP = 8
EDGE = 24
VM = pl.BlockSpec(memory_space=pltpu.VMEM)
SM = pl.BlockSpec(memory_space=pltpu.SMEM)
HB = pl.BlockSpec(memory_space=pltpu.HBM)
F32 = jnp.float32
BF16 = jnp.bfloat16


def limit(mib):
    return pltpu.CompilerParams(vmem_limit_bytes=mib * 2**20)


def cost(flops):
    return pl.CostEstimate(flops=flops, bytes_accessed=2**10, transcendentals=0)


def largest_divisor(steps, most):
    return max(u for u in range(1, most + 1) if steps % u == 0)


def in_vmem(value):
    return pltpu.with_memory_space_constraint(value, pltpu.VMEM)


def in_hbm(value):
    return pltpu.with_memory_space_constraint(value, pltpu.HBM)


def prepare_kernel(starts, up, slots, edge_up, smem_starts, sems, *, count):
    copies = [pltpu.make_async_copy(starts, smem_starts, sems.at[2])]
    for side, first in enumerate((0, count - EDGE)):
        copies.append(pltpu.make_async_copy(up.at[pl.ds(first, EDGE)], edge_up.at[side], sems.at[side]))
    for copy in copies:
        copy.start()
    first_block = lax.axis_index("weight") * count
    lanes = lax.broadcasted_iota(jnp.int32, slots.shape, 1)
    place = first_block + lax.broadcasted_iota(jnp.int32, slots.shape, 0) * 128 + lanes
    row = jnp.zeros(slots.shape, jnp.int32)
    first_row, enters, leaves = 0, 1, 1
    copies[0].wait()
    for f in range(1, smem_starts.shape[0]):
        start = smem_starts[f]
        row += (start <= place).astype(jnp.int32)
        first_row += (start <= first_block).astype(jnp.int32)
        enters = jnp.where(start == first_block, 0, enters)
        leaves = jnp.where(start == first_block + count, 0, leaves)
    enters = jnp.where(first_block == 0, 0, enters)
    flag_row = lax.broadcasted_iota(jnp.int32, slots.shape, 0) == slots.shape[0] - 1
    slots[...] = jnp.where(flag_row, jnp.where(lanes == 0, enters, leaves), row - first_row)
    for copy in copies[1:]:
        copy.wait()


def slot_of(slots, block):
    if isinstance(block, int):
        return slots[block // 128, block % 128]
    return slots[lax.shift_right_logical(block, 7), lax.bitwise_and(block, 127)]


def left_operand(slots, cols, by_col, first):
    none = by_col.shape[0] - 1
    even, odd = [], []
    for q in range(GROUP):
        col, is_odd = cols[first + q], (slot_of(slots, first + q) & 1) == 1
        even.append(by_col[jnp.where(is_odd, none, col)])
        odd.append(by_col[jnp.where(is_odd, col, none)])
    return jnp.concatenate([jnp.concatenate(even, axis=1), jnp.concatenate(odd, axis=1)], axis=0)


def slots_met(slots, first):
    slot = slot_of(slots, first)
    return slot + (slot & 1), slot | 1


def silu_gate(gate, up):
    return (gate * (0.5 * jnp.tanh(0.5 * gate) + 0.5) * up).astype(BF16)


def edge_groups(count):
    return [(side, k, first + k * GROUP) for side, first in ((0, 0), (1, count - EDGE)) for k in range(EDGE // GROUP)]


def group_sums(slots, cols, by_col, weights, first):
    left = left_operand(slots, cols, by_col, first)
    right = weights.reshape(GROUP * 128, 128)
    return jnp.dot(left, right, preferred_element_type=F32)


def add_group(slots, first, part, sums):
    rows = part.shape[0] // 2
    at_even, at_odd = slots_met(slots, first)
    old_even, old_odd = sums[at_even], sums[at_odd]
    sums[at_even] = old_even + part[:rows]
    sums[at_odd] = old_odd + part[rows:]


def add_rows(slots, cols, by_col, weights, sums, groups, unroll):
    def step(it, carry):
        for j in range(unroll):
            first = (groups[0] + it * unroll + j) * GROUP
            add_group(slots, first, group_sums(slots, cols, by_col, weights[pl.ds(first, GROUP)], first), sums)
        return carry

    lax.fori_loop(0, (groups[1] - groups[0]) // unroll, step, 0)


def gate_kernel(slots, cols, gate, *refs, unroll):
    pieces, (by_col, sums, whole) = refs[:-3], refs[-3:]
    col_blocks, rows = by_col.shape[0] - 1, by_col.shape[1]
    me = lax.axis_index("weight")
    for distance, piece in enumerate(pieces):
        whole[lax.bitwise_xor(me, distance)] = piece[0]
    merged = whole[...].reshape(rows, col_blocks * 128)
    for c in range(col_blocks):
        by_col[c] = merged[:, c * 128 : (c + 1) * 128]
    by_col[col_blocks] = jnp.zeros((rows, 128), BF16)
    sums[...] = jnp.zeros_like(sums)
    add_rows(slots, cols, by_col, gate, sums, (0, cols.shape[0] // GROUP), unroll)


def edge_kernel(slots, cols, by_col, edge_up, gate_sums, edge_sums, to_inner, to_outer):
    rows = by_col.shape[1]
    count = cols.shape[0]
    totals = [jnp.zeros((rows, 128), F32)] * 2
    shared = (0, slot_of(slots, count - 1))
    for side, k, first in edge_groups(count):
        weights = edge_up[side, k * GROUP : (k + 1) * GROUP]
        part = group_sums(slots, cols, by_col, weights, first)
        edge_sums[side, k] = part
        at_even, at_odd = slots_met(slots, first)
        totals[side] += jnp.where(at_even == shared[side], part[:rows], 0.0)
        totals[side] += jnp.where(at_odd == shared[side], part[rows:], 0.0)
    last_flag = slots.shape[0] - 1
    parts = []
    for side in (0, 1):
        both = jnp.concatenate([gate_sums[shared[side]], totals[side]], axis=1)
        parts.append(jnp.where(slots[last_flag, side] == 1, both, 0.0).astype(BF16))
    is_odd = (lax.axis_index("weight") & 1) == 1
    to_inner[...] = jnp.where(is_odd, parts[0], parts[1])
    to_outer[...] = jnp.where(is_odd, parts[1], parts[0])


def up_kernel(slots, cols, by_col, up, edge_sums, gate_sums, hidden, edges, sums, *, unroll):
    count = cols.shape[0]
    sums[...] = jnp.zeros_like(sums)
    for side, k, first in edge_groups(count):
        add_group(slots, first, edge_sums[side, k], sums)
    add_rows(slots, cols, by_col, up, sums, (EDGE // GROUP, (count - EDGE) // GROUP), unroll)
    hidden[...] = silu_gate(gate_sums[...], sums[...])
    for side, slot in enumerate((0, slot_of(slots, count - 1))):
        edges[side, 0] = gate_sums[slot]
        edges[side, 1] = sums[slot]


def down_kernel(slots, cols, hidden, edges, from_inner, from_outer, down, *refs, unroll):
    outs, (rows_in, sums) = refs[:-2], refs[-2:]
    size = len(outs)
    count = cols.shape[0]
    rows = hidden.shape[1]
    col_blocks = sums.shape[1]
    rows_in[...] = hidden[...]
    me = lax.axis_index("weight")
    is_odd = (me & 1) == 1
    inner, outer = from_inner[...].astype(F32), from_outer[...].astype(F32)
    before, after = jnp.where(is_odd, inner, outer), jnp.where(is_odd, outer, inner)
    for side, slot, part in ((0, 0, before), (1, slot_of(slots, count - 1), after)):
        rows_in[slot] = silu_gate(edges[side, 0] + part[:, :128], edges[side, 1] + part[:, 128:])
    sums[...] = jnp.zeros_like(sums)

    def step(it, carry):
        for j in range(unroll):
            first = (it * unroll + j) * GROUP
            slot = slot_of(slots, first)
            left = jnp.concatenate([rows_in[slot + (slot & 1)], rows_in[slot | 1]], axis=0)
            right = jnp.concatenate([down[first + q] for q in range(GROUP)], axis=1)
            part = jnp.dot(left, right, preferred_element_type=F32)
            for half in range(0, GROUP, 4):
                at = [(slot_of(slots, first + q) & 1, cols[first + q]) for q in range(half, half + 4)]
                old = [sums[odd, col] for odd, col in at]
                for q, (odd, col) in enumerate(at):
                    term = part[:, (half + q) * 128 : (half + q + 1) * 128]
                    sums[odd, col] = old[q] + jnp.where(odd == 1, term[rows:], term[:rows])
        return carry

    lax.fori_loop(0, count // GROUP // unroll, step, 0)
    share = col_blocks // size
    for distance, out in enumerate(outs):
        first = lax.bitwise_xor(me, distance) * share
        for c in range(share):
            total = sums[0, first + c] + sums[1, first + c]
            out[:, c * 128 : (c + 1) * 128] = total.astype(out.dtype)


def per_device(tokens, gate_blocks, up_blocks, down_blocks, row_starts, gate_cols, down_cols):
    count, width, _ = gate_blocks.shape
    model_width = tokens.shape[2]
    col_blocks = model_width // width
    size = lax.axis_size("weight")
    slab = tokens.shape[1]
    rows = size * slab
    row_slots = (count - 1) // GROUP + 3

    def swap(value, distance):
        return lax.ppermute(value, "weight", [(d, d ^ distance) for d in range(size)])

    order = list(range(2, size)) + [1]
    arrived = {distance: swap(tokens, distance) for distance in order}
    pieces = [tokens] + [arrived[distance] for distance in range(1, size)]
    slot_rows = -(-count // 128) + 1
    slots, edge_up = pl.pallas_call(
        functools.partial(prepare_kernel, count=count),
        out_shape=(
            jax.ShapeDtypeStruct((slot_rows, 128), jnp.int32),
            pltpu.VMEM((2, EDGE, width, width), BF16),
        ),
        in_specs=[HB, HB],
        out_specs=(VM, VM),
        scratch_shapes=[pltpu.SMEM(row_starts.shape, jnp.int32), pltpu.SemaphoreType.DMA((3,))],
        compiler_params=limit(4),
        cost_estimate=cost(2**33),
        name="prepare",
    )(in_hbm(row_starts), in_hbm(up_blocks))
    unroll = largest_divisor(count // GROUP, 28)
    by_col, gate_sums = pl.pallas_call(
        functools.partial(gate_kernel, unroll=unroll),
        out_shape=(
            pltpu.VMEM((col_blocks + 1, rows, width), BF16),
            pltpu.VMEM((row_slots, rows, width), F32),
        ),
        in_specs=[SM, SM] + [VM] * (size + 1),
        out_specs=(VM, VM),
        scratch_shapes=[pltpu.VMEM((size, slab, model_width), BF16)],
        compiler_params=limit(8),
        cost_estimate=cost(2**20),
        name="gate",
    )(slots, gate_cols, in_vmem(gate_blocks), *pieces)
    edge_sums, to_inner, to_outer = pl.pallas_call(
        edge_kernel,
        out_shape=(
            pltpu.VMEM((2, EDGE // GROUP, 2 * rows, width), F32),
            jax.ShapeDtypeStruct((rows, 2 * width), BF16),
            jax.ShapeDtypeStruct((rows, 2 * width), BF16),
        ),
        in_specs=[SM, SM, VM, VM, VM],
        out_specs=(VM, VM, VM),
        compiler_params=limit(4),
        cost_estimate=cost(2**20),
        name="edges",
    )(slots, gate_cols, in_vmem(by_col), edge_up, in_vmem(gate_sums))
    outer_pairs = [(d, (d + 1 if d % 2 else d - 1) % size) for d in range(size)]
    from_outer = lax.ppermute(to_outer, "weight", outer_pairs)
    from_inner = swap(to_inner, 1)
    hidden, edges = pl.pallas_call(
        functools.partial(up_kernel, unroll=largest_divisor((count - 2 * EDGE) // GROUP, 28)),
        out_shape=(
            pltpu.VMEM((row_slots, rows, width), BF16),
            pltpu.VMEM((2, 2, rows, width), F32),
        ),
        in_specs=[SM, SM, VM, VM, VM, VM],
        out_specs=(VM, VM),
        scratch_shapes=[pltpu.VMEM((row_slots, rows, width), F32)],
        compiler_params=limit(8),
        cost_estimate=cost(2**20),
        name="up",
    )(slots, gate_cols, in_vmem(by_col), in_vmem(up_blocks), in_vmem(edge_sums), in_vmem(gate_sums))
    outs = pl.pallas_call(
        functools.partial(down_kernel, unroll=unroll),
        out_shape=tuple(
            jax.ShapeDtypeStruct((rows, model_width // size), BF16 if distance else F32)
            for distance in range(size)
        ),
        in_specs=[SM, SM] + [VM] * 5,
        out_specs=(VM,) * size,
        scratch_shapes=[
            pltpu.VMEM((row_slots, rows, width), BF16),
            pltpu.VMEM((2, col_blocks, rows, width), F32),
        ],
        compiler_params=limit(8),
        cost_estimate=cost(2**20),
        name="down",
    )(slots, down_cols, in_vmem(hidden), in_vmem(edges), from_inner, from_outer, in_vmem(down_blocks))
    received = {distance: swap(outs[distance], distance) for distance in order}
    total = outs[0]
    for distance in order:
        total = total + received[distance].astype(F32)
    return total.astype(BF16).reshape(size, slab, model_width // size)


def solution(mesh):
    in_specs = (
        P("weight", ("groups", "dp"), None),
        P("weight", None, None),
        P("weight", None, None),
        P("weight", None, None),
        P(),
        P("weight"),
        P("weight"),
    )
    out_specs = P(None, ("groups", "dp"), "weight")
    return jax.shard_map(
        per_device, mesh=mesh, in_specs=in_specs, out_specs=out_specs, check_vma=False
    )
```

```python
import functools

import jax
import jax.numpy as jnp
from jax import lax
from jax.experimental import pallas as pl
from jax.experimental.pallas import tpu as pltpu
from jax.sharding import PartitionSpec as P

GROUP = 8
EDGE = 24
VM = pl.BlockSpec(memory_space=pltpu.VMEM)
SM = pl.BlockSpec(memory_space=pltpu.SMEM)
HB = pl.BlockSpec(memory_space=pltpu.HBM)
F32 = jnp.float32
BF16 = jnp.bfloat16


def limit(mib):
    return pltpu.CompilerParams(vmem_limit_bytes=mib * 2**20)


def cost(flops):
    return pl.CostEstimate(flops=flops, bytes_accessed=2**10, transcendentals=0)


def largest_divisor(steps, most):
    return max(u for u in range(1, most + 1) if steps % u == 0)


def in_vmem(value):
    return pltpu.with_memory_space_constraint(value, pltpu.VMEM)


def in_smem(value):
    return pltpu.with_memory_space_constraint(value, pltpu.SMEM)


def in_hbm(value):
    return pltpu.with_memory_space_constraint(value, pltpu.HBM)


def prepare_kernel(starts, slots, smem_starts, sem, *, count):
    copy = pltpu.make_async_copy(starts, smem_starts, sem)
    copy.start()
    first_block = lax.axis_index("weight") * count
    lanes = lax.broadcasted_iota(jnp.int32, slots.shape, 1)
    place = first_block + lax.broadcasted_iota(jnp.int32, slots.shape, 0) * 128 + lanes
    row = jnp.zeros(slots.shape, jnp.int32)
    first_row, enters, leaves = 0, 1, 1
    copy.wait()
    for f in range(1, smem_starts.shape[0]):
        start = smem_starts[f]
        row += (start <= place).astype(jnp.int32)
        first_row += (start <= first_block).astype(jnp.int32)
        enters = jnp.where(start == first_block, 0, enters)
        leaves = jnp.where(start == first_block + count, 0, leaves)
    enters = jnp.where(first_block == 0, 0, enters)
    flag_row = lax.broadcasted_iota(jnp.int32, slots.shape, 0) == slots.shape[0] - 1
    slots[...] = jnp.where(flag_row, jnp.where(lanes == 0, enters, leaves), row - first_row)


def slot_of(slots, block):
    if isinstance(block, int):
        return slots[block // 128, block % 128]
    return slots[lax.shift_right_logical(block, 7), lax.bitwise_and(block, 127)]


def left_operand(slots, cols, by_col, first):
    none = by_col.shape[0] - 1
    even, odd = [], []
    for q in range(GROUP):
        col, is_odd = cols[first + q], (slot_of(slots, first + q) & 1) == 1
        even.append(by_col[jnp.where(is_odd, none, col)])
        odd.append(by_col[jnp.where(is_odd, col, none)])
    return jnp.concatenate([jnp.concatenate(even, axis=1), jnp.concatenate(odd, axis=1)], axis=0)


def slots_met(slots, first):
    slot = slot_of(slots, first)
    return slot + (slot & 1), slot | 1


def silu_gate(gate, up):
    return (gate * (0.5 * jnp.tanh(0.5 * gate) + 0.5) * up).astype(BF16)


def edge_groups(count):
    return [(side, k, first + k * GROUP) for side, first in ((0, 0), (1, count - EDGE)) for k in range(EDGE // GROUP)]


def group_sums(slots, cols, by_col, weights, first):
    left = left_operand(slots, cols, by_col, first)
    right = weights.reshape(GROUP * 128, 128)
    return jnp.dot(left, right, preferred_element_type=F32)


def add_group(slots, first, part, sums):
    rows = part.shape[0] // 2
    at_even, at_odd = slots_met(slots, first)
    old_even, old_odd = sums[at_even], sums[at_odd]
    sums[at_even] = old_even + part[:rows]
    sums[at_odd] = old_odd + part[rows:]


def add_rows(slots, cols, by_col, weights, sums, groups, unroll):
    def step(it, carry):
        for j in range(unroll):
            first = (groups[0] + it * unroll + j) * GROUP
            add_group(slots, first, group_sums(slots, cols, by_col, weights[pl.ds(first, GROUP)], first), sums)
        return carry

    lax.fori_loop(0, (groups[1] - groups[0]) // unroll, step, 0)


def gate_kernel(slots, cols, gate, up, *refs, unroll):
    pieces, (by_col, sums, edge_up, whole, sems) = refs[:-5], refs[-5:]
    count = cols.shape[0]
    copies = [
        pltpu.make_async_copy(up.at[pl.ds(first, EDGE)], edge_up.at[side], sems.at[side])
        for side, first in enumerate((0, count - EDGE))
    ]
    for copy in copies:
        copy.start()
    col_blocks, rows = by_col.shape[0] - 1, by_col.shape[1]
    me = lax.axis_index("weight")
    for distance, piece in enumerate(pieces):
        whole[lax.bitwise_xor(me, distance)] = piece[0]
    merged = whole[...].reshape(rows, col_blocks * 128)
    for c in range(col_blocks):
        by_col[c] = merged[:, c * 128 : (c + 1) * 128]
    by_col[col_blocks] = jnp.zeros((rows, 128), BF16)
    sums[...] = jnp.zeros_like(sums)
    add_rows(slots, cols, by_col, gate, sums, (0, count // GROUP), unroll)
    for copy in copies:
        copy.wait()


def edge_kernel(slots, cols, by_col, edge_up, gate_sums, edge_sums, to_inner, to_outer):
    rows = by_col.shape[1]
    count = cols.shape[0]
    totals = [jnp.zeros((rows, 128), F32)] * 2
    shared = (0, slot_of(slots, count - 1))
    for side, k, first in edge_groups(count):
        weights = edge_up[side, k * GROUP : (k + 1) * GROUP]
        part = group_sums(slots, cols, by_col, weights, first)
        edge_sums[side, k] = part
        at_even, at_odd = slots_met(slots, first)
        totals[side] += jnp.where(at_even == shared[side], part[:rows], 0.0)
        totals[side] += jnp.where(at_odd == shared[side], part[rows:], 0.0)
    last_flag = slots.shape[0] - 1
    parts = []
    for side in (0, 1):
        both = jnp.concatenate([gate_sums[shared[side]], totals[side]], axis=1)
        parts.append(jnp.where(slots[last_flag, side] == 1, both, 0.0).astype(BF16))
    is_odd = (lax.axis_index("weight") & 1) == 1
    to_inner[...] = jnp.where(is_odd, parts[0], parts[1])
    to_outer[...] = jnp.where(is_odd, parts[1], parts[0])


def up_kernel(slots, cols, by_col, up, edge_sums, gate_sums, hidden, edges, sums, *, unroll):
    count = cols.shape[0]
    sums[...] = jnp.zeros_like(sums)
    for side, k, first in edge_groups(count):
        add_group(slots, first, edge_sums[side, k], sums)
    add_rows(slots, cols, by_col, up, sums, (EDGE // GROUP, (count - EDGE) // GROUP), unroll)
    hidden[...] = silu_gate(gate_sums[...], sums[...])
    for side, slot in enumerate((0, slot_of(slots, count - 1))):
        edges[side, 0] = gate_sums[slot]
        edges[side, 1] = sums[slot]


def down_kernel(slots, cols, hidden, edges, from_inner, from_outer, down, *refs, unroll):
    outs, (rows_in, sums) = refs[:-2], refs[-2:]
    size = len(outs)
    count = cols.shape[0]
    rows = hidden.shape[1]
    col_blocks = sums.shape[1]
    rows_in[...] = hidden[...]
    me = lax.axis_index("weight")
    is_odd = (me & 1) == 1
    inner, outer = from_inner[...].astype(F32), from_outer[...].astype(F32)
    before, after = jnp.where(is_odd, inner, outer), jnp.where(is_odd, outer, inner)
    for side, slot, part in ((0, 0, before), (1, slot_of(slots, count - 1), after)):
        rows_in[slot] = silu_gate(edges[side, 0] + part[:, :128], edges[side, 1] + part[:, 128:])
    sums[...] = jnp.zeros_like(sums)

    def step(it, carry):
        for j in range(unroll):
            first = (it * unroll + j) * GROUP
            slot = slot_of(slots, first)
            left = jnp.concatenate([rows_in[slot + (slot & 1)], rows_in[slot | 1]], axis=0)
            right = jnp.concatenate([down[first + q] for q in range(GROUP)], axis=1)
            part = jnp.dot(left, right, preferred_element_type=F32)
            for half in range(0, GROUP, 4):
                at = [(slot_of(slots, first + q) & 1, cols[first + q]) for q in range(half, half + 4)]
                old = [sums[odd, col] for odd, col in at]
                for q, (odd, col) in enumerate(at):
                    term = part[:, (half + q) * 128 : (half + q + 1) * 128]
                    sums[odd, col] = old[q] + jnp.where(odd == 1, term[rows:], term[:rows])
        return carry

    lax.fori_loop(0, count // GROUP // unroll, step, 0)
    share = col_blocks // size
    for distance, out in enumerate(outs):
        first = lax.bitwise_xor(me, distance) * share
        for c in range(share):
            total = sums[0, first + c] + sums[1, first + c]
            out[:, c * 128 : (c + 1) * 128] = total.astype(out.dtype)


def per_device(tokens, gate_blocks, up_blocks, down_blocks, row_starts, gate_cols, down_cols):
    count, width, _ = gate_blocks.shape
    model_width = tokens.shape[2]
    col_blocks = model_width // width
    size = lax.axis_size("weight")
    slab = tokens.shape[1]
    rows = size * slab
    row_slots = (count - 1) // GROUP + 3

    def swap(value, distance):
        return lax.ppermute(value, "weight", [(d, d ^ distance) for d in range(size)])

    order = list(range(2, size)) + [1]
    arrived = {distance: swap(tokens, distance) for distance in order}
    pieces = [tokens] + [arrived[distance] for distance in range(1, size)]
    slot_rows = -(-count // 128) + 1
    slots = pl.pallas_call(
        functools.partial(prepare_kernel, count=count),
        out_shape=jax.ShapeDtypeStruct((slot_rows, 128), jnp.int32),
        in_specs=[HB],
        out_specs=VM,
        scratch_shapes=[pltpu.SMEM(row_starts.shape, jnp.int32), pltpu.SemaphoreType.DMA(())],
        compiler_params=limit(2),
        cost_estimate=cost(2**36),
        name="prepare",
    )(in_hbm(row_starts))
    unroll = largest_divisor(count // GROUP, 28)
    by_col, gate_sums, edge_up = pl.pallas_call(
        functools.partial(gate_kernel, unroll=unroll),
        out_shape=(
            pltpu.VMEM((col_blocks + 1, rows, width), BF16),
            pltpu.VMEM((row_slots, rows, width), F32),
            pltpu.VMEM((2, EDGE, width, width), BF16),
        ),
        in_specs=[SM, SM, VM, HB] + [VM] * size,
        out_specs=(VM, VM, VM),
        scratch_shapes=[pltpu.VMEM((size, slab, model_width), BF16), pltpu.SemaphoreType.DMA((2,))],
        compiler_params=limit(8),
        cost_estimate=cost(2**20),
        name="gate",
    )(in_smem(slots), in_smem(gate_cols), in_vmem(gate_blocks), in_hbm(up_blocks), *pieces)
    edge_sums, to_inner, to_outer = pl.pallas_call(
        edge_kernel,
        out_shape=(
            pltpu.VMEM((2, EDGE // GROUP, 2 * rows, width), F32),
            jax.ShapeDtypeStruct((rows, 2 * width), BF16),
            jax.ShapeDtypeStruct((rows, 2 * width), BF16),
        ),
        in_specs=[SM, SM, VM, VM, VM],
        out_specs=(VM, VM, VM),
        compiler_params=limit(4),
        cost_estimate=cost(2**20),
        name="edges",
    )(in_smem(slots), in_smem(gate_cols), in_vmem(by_col), in_vmem(edge_up), in_vmem(gate_sums))
    outer_pairs = [(d, (d + 1 if d % 2 else d - 1) % size) for d in range(size)]
    from_outer = lax.ppermute(to_outer, "weight", outer_pairs)
    from_inner = swap(to_inner, 1)
    hidden, edges = pl.pallas_call(
        functools.partial(up_kernel, unroll=largest_divisor((count - 2 * EDGE) // GROUP, 28)),
        out_shape=(
            pltpu.VMEM((row_slots, rows, width), BF16),
            pltpu.VMEM((2, 2, rows, width), F32),
        ),
        in_specs=[SM, SM, VM, VM, VM, VM],
        out_specs=(VM, VM),
        scratch_shapes=[pltpu.VMEM((row_slots, rows, width), F32)],
        compiler_params=limit(8),
        cost_estimate=cost(2**20),
        name="up",
    )(in_smem(slots), in_smem(gate_cols), in_vmem(by_col), in_vmem(up_blocks), in_vmem(edge_sums), in_vmem(gate_sums))
    outs = pl.pallas_call(
        functools.partial(down_kernel, unroll=unroll),
        out_shape=tuple(
            jax.ShapeDtypeStruct((rows, model_width // size), BF16 if distance else F32)
            for distance in range(size)
        ),
        in_specs=[SM, SM] + [VM] * 5,
        out_specs=(VM,) * size,
        scratch_shapes=[
            pltpu.VMEM((row_slots, rows, width), BF16),
            pltpu.VMEM((2, col_blocks, rows, width), F32),
        ],
        compiler_params=limit(8),
        cost_estimate=cost(2**20),
        name="down",
    )(in_smem(slots), in_smem(down_cols), in_vmem(hidden), in_vmem(edges), from_inner, from_outer, in_vmem(down_blocks))
    received = {distance: swap(outs[distance], distance) for distance in order}
    total = outs[0]
    for distance in order:
        total = total + received[distance].astype(F32)
    return total.astype(BF16).reshape(size, slab, model_width // size)


def solution(mesh):
    in_specs = (
        P("weight", ("groups", "dp"), None),
        P("weight", None, None),
        P("weight", None, None),
        P("weight", None, None),
        P(),
        P("weight"),
        P("weight"),
    )
    out_specs = P(None, ("groups", "dp"), "weight")
    return jax.shard_map(
        per_device, mesh=mesh, in_specs=in_specs, out_specs=out_specs, check_vma=False
    )
```
